32 devices in a mesh: gx: 8 (over y, x, core), gy: 4 (over z).
Axes of the slice: x: 2, y: 2, z: 4, core: 2. Of those that a mesh axis runs over, the one named last changes fastest.
Arguments:
- control: float32 [6, 2048, 1024], P(None, 'gy', 'gx'), may hold values from -6 to 6
- field_scale: float32 [6], replicated, may hold values from 0.5 to 2
- water_depth: float32 [2048, 1024], P('gy', 'gx'), may hold values from 0.5 to 4
- bed_mobility: float32 [2048, 1024], P('gy', 'gx'), may hold values from 0.1 to 1
- footprint: int32 [32, 32, 8], P(('gx', 'gy')), may hold values from 0 to 511
- instrument: int32 [32, 32, 8], P(('gx', 'gy')), may hold values from 0 to 1
- live_counts: int32 [32, 32], P(('gx', 'gy')), may hold values from 0 to 8, as said below
- observed: float32 [32, 32, 8, 128], P(('gx', 'gy')), may hold values from -6 to 6
- obs_precision: float32 [2, 128, 128], replicated, may hold values from -0.001 to 0.012, as said below
Outputs:
- gradient: float32 [6, 2048, 1024], P(None, 'gy', 'gx')
The draws below stay inside these ranges and needn't reach their ends.
Inputs may be any that keep to these rules, and one draw needn't show every extreme that they name: `live_counts`: every owner has at least one source device whose 8 slots are all live. `obs_precision`: Symmetric; every diagonal entry exceeds the sum of the magnitudes of the other entries of its row.
All inputs are finite; a program needn't handle non-finite values.
Results may differ from the reference program's by a relative error of at most 0.0001.
Values sent between devices are 32-bit elements; how exact they have to be, the bound alone decides.
A program may use at most 64 MiB of HBM per device.

```python
import math
import jax
import jax.numpy as jnp
from jax import lax

F = 6
HALF = 128
BLK = 128
STEPS = 3
CAP = 8
CX = 128
CY = 512
NX = 1024
NY = 2048
OWNERS = 32
N_GY = 4


def draw_live_counts(key, part):
    key_busy = jax.random.fold_in(key, 11)
    key_heavy = jax.random.fold_in(key, 12)
    key_light = jax.random.fold_in(key, 13)
    key_full = jax.random.fold_in(key, 14)
    busy_owner = jax.random.randint(key_busy, (OWNERS, 1), 0, 4) == 0
    heavy_load = jax.random.randint(key_heavy, (OWNERS, OWNERS), CAP // 2, CAP + 1)
    light_load = jax.random.randint(key_light, (OWNERS, OWNERS), 0, CAP // 2 + 1)
    base_load = jnp.where(busy_owner, heavy_load, light_load)
    chosen = jax.random.randint(key_full, (OWNERS, 1), 0, OWNERS)
    full_slot = jnp.arange(OWNERS, dtype=jnp.int32)[None, :] == chosen
    return jnp.where(full_slot, CAP, base_load).astype(jnp.int32)


def draw_obs_precision(key, part):
    key_off = jax.random.fold_in(key, 21)
    key_diag = jax.random.fold_in(key, 22)
    random_off = jax.random.uniform(key_off, (2, BLK, BLK), jnp.float32, -1.0, 1.0)
    mirrored = 0.5 * (random_off + jnp.swapaxes(random_off, 1, 2)) / BLK
    diagonal = jax.random.uniform(key_diag, (2, BLK, 1), jnp.float32, 2.0, 3.0)
    eye_mask = jnp.arange(BLK)[:, None] == jnp.arange(BLK)[None, :]
    return (jnp.where(eye_mask[None], diagonal, mirrored) / 256.0).astype(jnp.float32)


def plant(drawn, stream_key, least, largest):
    spot = [jax.random.randint(jax.random.fold_in(stream_key, axis), (), 0, length) for axis, length in enumerate(drawn.shape)]
    main_axis = drawn.shape.index(max(drawn.shape))
    next_to = spot[:main_axis] + [(spot[main_axis] + 1) % drawn.shape[main_axis]] + spot[main_axis + 1:]
    return drawn.at[tuple(spot)].set(least).at[tuple(next_to)].set(largest)


def shard_levels(own_key, dims, shards, low, largest):
    gain, own = 1.0, jax.random.fold_in(own_key, 6)
    for axis_at, parts in shards:
        draws = jnp.exp(jax.random.uniform(jax.random.fold_in(own, axis_at), (parts,), jnp.float32, low / len(shards), largest / len(shards)))
        gain = gain * jnp.repeat(draws, dims[axis_at] // parts).reshape([-1 if axis == axis_at else 1 for axis in range(len(dims))])
    return gain


def bell_draw(stream_key, shape, scale, most, shards=(), held_as=jnp.bfloat16):
    level = shard_levels(stream_key, shape, shards, -0.22, 0.18) if shards else 1.0
    drawn = jax.random.normal(stream_key, shape, jnp.float32) * scale * level
    return jnp.minimum(jnp.maximum(drawn, -most), most).astype(held_as)


def setup_inputs(seed: int = 0) -> dict:
    splits = jax.random.split(jax.random.key(seed), 10)
    return {
        "control": bell_draw(splits[0], (F, NY, NX), 1.0, 6.0, ((1, 4), (2, 8)), jnp.float32),
        "field_scale": jnp.clip(jnp.exp(jax.random.uniform(splits[1], (F,), jnp.float32, math.log(0.5), math.log(2.0))), 0.5, 2.0),
        "water_depth": jnp.clip(jnp.exp(math.log(4.0) - 2.0794415 * jax.random.uniform(splits[2], (NY, NX), jnp.float32) ** shard_levels(splits[2], (NY, NX), ((0, 4), (1, 8)), -0.2, 0.2)), 0.5, 4.0),
        "bed_mobility": jnp.clip(jnp.exp(math.log(1.0) - 2.3025851 * jax.random.uniform(splits[3], (NY, NX), jnp.float32) ** shard_levels(splits[3], (NY, NX), ((0, 4), (1, 8)), -0.2, 0.2)), 0.1, 1.0),
        "footprint": plant(jax.random.randint(splits[4], (OWNERS, OWNERS, CAP), 0, CY * CX // BLK), jax.random.fold_in(splits[4], 1), 0, (CY * CX // BLK) - 1).astype(jnp.int32),
        "instrument": plant(jax.random.randint(splits[5], (OWNERS, OWNERS, CAP), 0, 2), jax.random.fold_in(splits[5], 1), 0, 1).astype(jnp.int32),
        "live_counts": draw_live_counts(jax.random.fold_in(splits[9], 71), 0),
        "observed": bell_draw(splits[7], (OWNERS, OWNERS, CAP, BLK), 1.0, 6.0, ((0, 32),), jnp.float32),
        "obs_precision": draw_obs_precision(jax.random.fold_in(splits[9], 71), 0),
    }


TIME_STEP = 0.2
GRAVITY = 1.0
FRICTION = 0.5
DIFFUSION = (0.4, 0.25)
SETTLING = (0.5, 0.2)

def band_table():
    window = jnp.arange(3 * HALF, dtype=jnp.int32)[:, None]
    column = jnp.arange(HALF, dtype=jnp.int32)[None, :]
    offsets = (window - column - HALF).astype(jnp.float32)
    corr_length = HALF / 2.0
    inside = jnp.abs(offsets) <= HALF
    kernel = jnp.where(inside, jnp.exp(-offsets * offsets / (2.0 * corr_length * corr_length)), 0.0)
    tap_offsets = jnp.arange(-HALF, HALF + 1, dtype=jnp.int32).astype(jnp.float32)
    norm_sum = jnp.sqrt(jnp.sum(jnp.exp(-tap_offsets * tap_offsets / (corr_length * corr_length))))
    return kernel / norm_sum

def column_pass(padded, kernel):
    channels, extent, breadth = padded.shape
    inner_count = breadth // HALF - 2
    blocks = padded.reshape(channels, extent, inner_count + 2, HALF)
    result = jnp.zeros((channels, extent, inner_count, HALF), jnp.float32)
    for offset in range(3):
        result = result + jnp.einsum('frtw,wk->frtk', blocks[:, :, offset:offset + inner_count], kernel[offset * HALF:(offset + 1) * HALF], precision=lax.Precision.HIGHEST)
    return result.reshape(channels, extent, inner_count * HALF)

def row_pass(padded, kernel):
    channels, extent, breadth = padded.shape
    inner_count = extent // HALF - 2
    blocks = padded.reshape(channels, inner_count + 2, HALF, breadth)
    result = jnp.zeros((channels, inner_count, HALF, breadth), jnp.float32)
    for offset in range(3):
        result = result + jnp.einsum('ftwc,wk->ftkc', blocks[:, offset:offset + inner_count], kernel[offset * HALF:(offset + 1) * HALF], precision=lax.Precision.HIGHEST)
    return result.reshape(channels, inner_count * HALF, breadth)

def correlate(fields, kernel):
    wide = column_pass(jnp.pad(fields, ((0, 0), (0, 0), (HALF, HALF))), kernel)
    return row_pass(jnp.pad(wide, ((0, 0), (HALF, HALF), (0, 0))), kernel)

def slope_x(padded):
    return 0.5 * (padded[:, 1:-1, 2:] - padded[:, 1:-1, :-2])

def slope_y(padded):
    return 0.5 * (padded[:, 2:, 1:-1] - padded[:, :-2, 1:-1])

def laplace(padded):
    return padded[:, 2:, 1:-1] + padded[:, :-2, 1:-1] + padded[:, 1:-1, 2:] + padded[:, 1:-1, :-2] - 4.0 * padded[:, 1:-1, 1:-1]

def pad_edges(stacked):
    return jnp.pad(stacked, ((0, 0), (1, 1), (1, 1)))

def flow_step(fields, water_depth, bed_mobility):
    height, speed_x, speed_y, bed_level, silt_one, silt_two = (fields[0], fields[1], fields[2], fields[3], fields[4], fields[5])
    fluxes = jnp.stack([water_depth * speed_x, water_depth * speed_y, bed_mobility * speed_x, bed_mobility * speed_y, silt_one, silt_two])
    padded = pad_edges(fluxes)
    along_x = slope_x(padded[:4])
    along_y = slope_y(padded[:4])
    spread = laplace(padded[4:])
    height_new = height - TIME_STEP * (along_x[0] + along_y[1])
    bed_new = bed_level - TIME_STEP * (along_x[2] + along_y[3]) + TIME_STEP * (SETTLING[0] * silt_one + SETTLING[1] * silt_two)
    silt_one_new = silt_one + TIME_STEP * DIFFUSION[0] * spread[0] - TIME_STEP * SETTLING[0] * silt_one
    silt_two_new = silt_two + TIME_STEP * DIFFUSION[1] * spread[1] - TIME_STEP * SETTLING[1] * silt_two
    surface_pad = pad_edges((height_new + bed_new)[None])
    speed_x_new = (1.0 - TIME_STEP * FRICTION) * speed_x - TIME_STEP * GRAVITY * slope_x(surface_pad)[0]
    speed_y_new = (1.0 - TIME_STEP * FRICTION) * speed_y - TIME_STEP * GRAVITY * slope_y(surface_pad)[0]
    return jnp.stack([height_new, speed_x_new, speed_y_new, bed_new, silt_one_new, silt_two_new])

def reference(control, field_scale, water_depth, bed_mobility, footprint, instrument, live_counts, observed, obs_precision):
    kernel = band_table()
    sources = jnp.arange(OWNERS, dtype=jnp.int32)
    column_base = sources // N_GY * CX
    row_base = sources % N_GY * CY
    segments = CX // BLK
    row_index = (row_base[:, None, None] + footprint // segments)[..., None]
    column_index = (column_base[:, None, None] + footprint % segments * BLK)[..., None] + jnp.arange(BLK, dtype=jnp.int32)

    def equivalents(control_in):
        fields = field_scale[:, None, None] * correlate(control_in, kernel)
        for _ in range(STEPS):
            fields = flow_step(fields, water_depth, bed_mobility)
        surface = jnp.swapaxes((fields[0] + fields[3])[row_index, column_index], 0, 1)
        bed_seen = jnp.swapaxes(fields[3][row_index, column_index], 0, 1)
        return jnp.where(instrument[..., None] == 0, surface, bed_seen)
    sensed, pullback = jax.vjp(equivalents, control)
    misfit = sensed - observed
    weighted_sar = jnp.einsum('qpcj,ij->qpci', misfit, obs_precision[0], precision=lax.Precision.HIGHEST)
    weighted_lidar = jnp.einsum('qpcj,ij->qpci', misfit, obs_precision[1], precision=lax.Precision.HIGHEST)
    live_mask = (jnp.arange(CAP, dtype=jnp.int32)[None, None, :] < live_counts[:, :, None])[..., None]
    weighted = jnp.where(live_mask, jnp.where(instrument[..., None] == 0, weighted_sar, weighted_lidar), 0.0)
    return control + pullback(weighted)[0]
```

```python
import functools

import jax
import jax.numpy as jnp
from jax import lax
from jax.experimental import pallas as pl
from jax.experimental.pallas import tpu as pltpu
from jax.sharding import PartitionSpec as P

HALF = 128
BLK = 128
STEPS = 3


TIME_STEP = 0.2
GRAVITY = 1.0
FRICTION = 0.5
DIFFUSION = (0.4, 0.25)
SETTLING = (0.5, 0.2)


def with_halo(block, sides, width):
    for axis, dim in sides:
        count = lax.axis_size(axis)
        forward = [(i, i + 1) for i in range(count - 1)]
        backward = [(target, source) for source, target in forward]
        low = lax.ppermute(
            lax.slice_in_dim(block, block.shape[dim] - width, None, axis=dim), axis, forward
        )
        high = lax.ppermute(lax.slice_in_dim(block, 0, width, axis=dim), axis, backward)
        block = jnp.concatenate([low, block, high], axis=dim)
    return block


def band_table():
    window = jnp.arange(3 * HALF, dtype=jnp.int32)[:, None]
    column = jnp.arange(HALF, dtype=jnp.int32)[None, :]
    offsets = (window - column - HALF).astype(jnp.float32)
    corr_length = HALF / 2.0
    inside = jnp.abs(offsets) <= HALF
    kernel = jnp.where(inside, jnp.exp(-offsets * offsets / (2.0 * corr_length * corr_length)), 0.0)
    tap_offsets = jnp.arange(-HALF, HALF + 1, dtype=jnp.int32).astype(jnp.float32)
    norm_sum = jnp.sqrt(jnp.sum(jnp.exp(-tap_offsets * tap_offsets / (corr_length * corr_length))))
    return kernel / norm_sum


def split(value):
    high = value.astype(jnp.bfloat16)
    return high, (value - high.astype(jnp.float32)).astype(jnp.bfloat16)


def mul(left, right):
    return jnp.dot(left, right, preferred_element_type=jnp.float32)


def mul_pair(left, right):
    return mul(left[0], right[0]) + mul(left[0], right[1]) + mul(left[1], right[0])


def neighbours(names, counts):
    found = []
    for axis, count in zip(names, counts):
        me = lax.axis_index(axis)
        found.append((axis, me - 1, me > 0))
        found.append((axis, me + 1, me < count - 1))
    return found


def greet(around):
    barrier = pltpu.get_barrier_semaphore()
    for axis, other, there in around:

        @pl.when(there)
        def _():
            pl.semaphore_signal(
                barrier, inc=1, device_id={axis: other}, device_id_type=pl.DeviceIdType.MESH
            )

    pl.semaphore_wait(barrier, sum(there.astype(jnp.int32) for _, _, there in around))


def correlate_kernel(
    counts, x_ref, taps_ref, out_ref, low_x, high_x, low_y, high_y, wide, high_ref, low_ref, send, recv
):
    fields, rows, cols = x_ref.shape
    around = neighbours(("gx", "gy"), counts)
    greet(around)

    def taps(index):
        part = pl.ds(index * HALF, HALF)
        return high_ref[part, :], low_ref[part, :]

    def copy(field, side):
        axis, other, _ = around[side]
        if side == 0:
            source, target = x_ref.at[field], high_x.at[field]
        elif side == 1:
            source, target = x_ref.at[field], low_x.at[field]
        elif side == 2:
            source, target = wide.at[field, pl.ds(0, HALF)], high_y.at[field]
        else:
            source, target = wide.at[field, pl.ds(rows - HALF, HALF)], low_y.at[field]
        return pltpu.make_async_remote_copy(
            src_ref=source,
            dst_ref=target,
            send_sem=send.at[side, field],
            recv_sem=recv.at[side, field],
            device_id={axis: other},
            device_id_type=pl.DeviceIdType.MESH,
        )

    def start_x(field, carry):
        for side in (0, 1):

            @pl.when(around[side][2])
            def _():
                copy(field, side).start()

        return carry

    lax.fori_loop(0, fields, start_x, 0)
    for there, halo in (
        (around[0][2], low_x),
        (around[1][2], high_x),
        (around[2][2], low_y),
        (around[3][2], high_y),
    ):

        @pl.when(jnp.logical_not(there))
        def _():
            halo[...] = jnp.zeros_like(halo)

    high_ref[...], low_ref[...] = split(taps_ref[...])

    def own(field, carry):
        wide[field] = mul_pair(split(x_ref[field]), taps(1))
        return carry

    lax.fori_loop(0, fields, own, 0)

    def columns(field, carry):
        @pl.when(around[0][2])
        def _():
            copy(field, 1).wait_recv()

        @pl.when(around[1][2])
        def _():
            copy(field, 0).wait_recv()

        wide[field] = (
            wide[field]
            + mul_pair(split(low_x[field]), taps(0))
            + mul_pair(split(high_x[field]), taps(2))
        )
        for side in (2, 3):

            @pl.when(around[side][2])
            def _():
                copy(field, side).start()

        pieces = [split(wide[field, pl.ds(t * HALF, HALF), :]) for t in range(rows // HALF)]
        for t, piece in enumerate(pieces):
            total = mul_pair(taps(1), piece)
            if t > 0:
                total = total + mul_pair(taps(2), pieces[t - 1])
            if t < len(pieces) - 1:
                total = total + mul_pair(taps(0), pieces[t + 1])
            out_ref[field, pl.ds(t * HALF, HALF), :] = total
        return carry

    lax.fori_loop(0, fields, columns, 0)

    def edges(field, carry):
        @pl.when(around[2][2])
        def _():
            copy(field, 3).wait_recv()

        @pl.when(around[3][2])
        def _():
            copy(field, 2).wait_recv()

        first, last = pl.ds(0, HALF), pl.ds(rows - HALF, HALF)
        out_ref[field, first, :] = out_ref[field, first, :] + mul_pair(taps(2), split(low_y[field]))
        out_ref[field, last, :] = out_ref[field, last, :] + mul_pair(taps(0), split(high_y[field]))
        for side in range(4):

            @pl.when(around[side][2])
            def _():
                copy(field, side).wait_send()

        return carry

    lax.fori_loop(0, fields, edges, 0)


def correlate(block, kernel, name):
    fields, rows, cols = block.shape
    counts = (lax.axis_size("gx"), lax.axis_size("gy"))
    full = pl.BlockSpec(memory_space=pltpu.VMEM)
    edge = pltpu.VMEM((fields, HALF, cols), jnp.float32)
    side = pltpu.VMEM((fields, rows, cols), jnp.float32)
    return pl.pallas_call(
        functools.partial(correlate_kernel, counts),
        out_shape=jax.ShapeDtypeStruct(block.shape, jnp.float32),
        in_specs=[full] * 2,
        out_specs=full,
        scratch_shapes=[
            side,
            side,
            edge,
            edge,
            side,
            pltpu.VMEM(kernel.shape, jnp.bfloat16),
            pltpu.VMEM(kernel.shape, jnp.bfloat16),
            pltpu.SemaphoreType.DMA((4, fields)),
            pltpu.SemaphoreType.DMA((4, fields)),
        ],
        compiler_params=pltpu.CompilerParams(
            collective_id=name, has_side_effects=True, vmem_limit_bytes=40 * 2**20
        ),
        cost_estimate=pl.CostEstimate(
            flops=36 * fields * rows * cols * HALF,
            bytes_accessed=8 * fields * rows * cols,
            transcendentals=0,
        ),
    )(block, kernel)


def observation_sums(rows, footprint, instrument, live_counts, observed):
    slots = footprint.shape[1]
    live = jnp.arange(slots, dtype=jnp.int32)[None, :] < live_counts[:, None]
    code = jnp.where(live, instrument + 1, 0).astype(jnp.float32)
    code = jnp.pad(code, ((0, 0), (0, BLK - slots)))[:, None, :]
    sent = jnp.concatenate([observed, code], axis=1)
    came = lax.all_to_all(sent, ("gx", "gy"), split_axis=0, concat_axis=0, tiled=True)
    values = came[:, :slots].reshape(-1, BLK)
    kinds = came[:, slots, :slots].reshape(-1)
    here = footprint.reshape(-1)[None, :] == jnp.arange(rows, dtype=jnp.int32)[:, None]
    sums = []
    for kind in (1.0, 2.0):
        picked = (here & (kinds == kind)[None, :]).astype(jnp.float32)
        sums.append(
            (
                jnp.sum(picked, axis=1, keepdims=True),
                jnp.dot(picked, values, precision=lax.Precision.HIGHEST),
            )
        )
    return sums


def slope_x(padded):
    return 0.5 * (padded[:, 1:-1, 2:] - padded[:, 1:-1, :-2])


def slope_y(padded):
    return 0.5 * (padded[:, 2:, 1:-1] - padded[:, :-2, 1:-1])


def laplace(padded):
    return (
        padded[:, 2:, 1:-1]
        + padded[:, :-2, 1:-1]
        + padded[:, 1:-1, 2:]
        + padded[:, 1:-1, :-2]
        - 4.0 * padded[:, 1:-1, 1:-1]
    )


def inside_grid(margin, rows, cols):
    row_ids = lax.axis_index("gy") * rows + jnp.arange(rows + 2 * margin, dtype=jnp.int32) - margin
    col_ids = lax.axis_index("gx") * cols + jnp.arange(cols + 2 * margin, dtype=jnp.int32) - margin
    row_ok = (row_ids >= 0) & (row_ids < rows * lax.axis_size("gy"))
    col_ok = (col_ids >= 0) & (col_ids < cols * lax.axis_size("gx"))
    return (row_ok[:, None] & col_ok[None, :]).astype(jnp.float32)


def trim(plane):
    return plane[1:-1, 1:-1]


def trim_two(plane):
    return plane[2:-2, 2:-2]


def region_step(fields, depth, mobility, inside):
    height, speed_x, speed_y, bed_level, silt_one, silt_two = (
        fields[0],
        fields[1],
        fields[2],
        fields[3],
        fields[4],
        fields[5],
    )
    fluxes = jnp.stack(
        [
            depth * speed_x,
            depth * speed_y,
            mobility * speed_x,
            mobility * speed_y,
            silt_one,
            silt_two,
        ]
    )
    along_x = slope_x(fluxes[:4])
    along_y = slope_y(fluxes[:4])
    spread = laplace(fluxes[4:])
    middle = trim(inside)
    height_new = (trim(height) - TIME_STEP * (along_x[0] + along_y[1])) * middle
    bed_new = (
        trim(bed_level)
        - TIME_STEP * (along_x[2] + along_y[3])
        + TIME_STEP * (SETTLING[0] * trim(silt_one) + SETTLING[1] * trim(silt_two))
    ) * middle
    silt_one_new = (
        trim(silt_one)
        + TIME_STEP * DIFFUSION[0] * spread[0]
        - TIME_STEP * SETTLING[0] * trim(silt_one)
    ) * middle
    silt_two_new = (
        trim(silt_two)
        + TIME_STEP * DIFFUSION[1] * spread[1]
        - TIME_STEP * SETTLING[1] * trim(silt_two)
    ) * middle
    surface = (height_new + bed_new)[None]
    core = trim_two(inside)
    speed_x_new = (
        (1.0 - TIME_STEP * FRICTION) * trim_two(speed_x) - TIME_STEP * GRAVITY * slope_x(surface)[0]
    ) * core
    speed_y_new = (
        (1.0 - TIME_STEP * FRICTION) * trim_two(speed_y) - TIME_STEP * GRAVITY * slope_y(surface)[0]
    ) * core
    return jnp.stack(
        [
            trim(height_new),
            speed_x_new,
            speed_y_new,
            trim(bed_new),
            trim(silt_one_new),
            trim(silt_two_new),
        ]
    )


def region_adjoint(adjoint, depth, mobility, inside):
    adj_height, adj_speed_x, adj_speed_y, adj_bed, adj_silt_one, adj_silt_two = (
        adjoint[0],
        adjoint[1],
        adjoint[2],
        adjoint[3],
        adjoint[4],
        adjoint[5],
    )
    adj_surface = (
        TIME_STEP * GRAVITY * (slope_x(adj_speed_x[None])[0] + slope_y(adj_speed_y[None])[0])
    )
    middle = trim(inside)
    height_mid = (trim(adj_height) + adj_surface) * middle
    bed_mid = (trim(adj_bed) + adj_surface) * middle
    levels = jnp.stack([height_mid, bed_mid, trim(adj_silt_one), trim(adj_silt_two)])
    grad_x = TIME_STEP * slope_x(levels[:2])
    grad_y = TIME_STEP * slope_y(levels[:2])
    spread = laplace(levels[2:])
    core = trim_two(inside)
    bed_core = trim(bed_mid)
    new_speed_x = (
        (1.0 - TIME_STEP * FRICTION) * trim_two(adj_speed_x)
        + trim_two(depth) * grad_x[0]
        + trim_two(mobility) * grad_x[1]
    ) * core
    new_speed_y = (
        (1.0 - TIME_STEP * FRICTION) * trim_two(adj_speed_y)
        + trim_two(depth) * grad_y[0]
        + trim_two(mobility) * grad_y[1]
    ) * core
    new_silt_one = (
        trim_two(adj_silt_one)
        + TIME_STEP * DIFFUSION[0] * spread[0]
        - TIME_STEP * SETTLING[0] * trim_two(adj_silt_one)
        + TIME_STEP * SETTLING[0] * bed_core
    ) * core
    new_silt_two = (
        trim_two(adj_silt_two)
        + TIME_STEP * DIFFUSION[1] * spread[1]
        - TIME_STEP * SETTLING[1] * trim_two(adj_silt_two)
        + TIME_STEP * SETTLING[1] * bed_core
    ) * core
    return jnp.stack(
        [trim(height_mid), new_speed_x, new_speed_y, bed_core, new_silt_one, new_silt_two]
    )


def on_device(
    control,
    field_scale,
    water_depth,
    bed_mobility,
    footprint,
    instrument,
    live_counts,
    observed,
    obs_precision,
):
    kernel = band_table()
    scales = field_scale[:, None, None]
    rows = water_depth.shape[0]
    cols = water_depth.shape[1]
    (count_sar, sum_sar), (count_lidar, sum_lidar) = observation_sums(
        rows, footprint[0], instrument[0], live_counts[0], observed[0]
    )
    fields = scales * correlate(control, kernel, 1)
    margin = 2 * STEPS
    stacked = jnp.concatenate([fields, water_depth[None], bed_mobility[None]])
    extended = with_halo(stacked, (("gx", 2), ("gy", 1)), margin)
    depth_wide = extended[6]
    mobility_wide = extended[7]
    inside_wide = inside_grid(margin, rows, cols)
    fields = extended[:6]
    depth_now, mobility_now, inside_now = (depth_wide, mobility_wide, inside_wide)
    for _ in range(STEPS):
        fields = region_step(fields, depth_now, mobility_now, inside_now)
        depth_now, mobility_now, inside_now = (
            trim_two(depth_now),
            trim_two(mobility_now),
            trim_two(inside_now),
        )
    misfit_sar = count_sar * (fields[0] + fields[3]) - sum_sar
    misfit_lidar = count_lidar * fields[3] - sum_lidar
    weighted_sar = jnp.einsum(
        "rj,ij->ri", misfit_sar, obs_precision[0], precision=lax.Precision.HIGHEST
    )
    weighted_lidar = jnp.einsum(
        "rj,ij->ri", misfit_lidar, obs_precision[1], precision=lax.Precision.HIGHEST
    )
    planes = jnp.stack([weighted_sar, weighted_sar + weighted_lidar])
    wide_planes = with_halo(planes, (("gx", 2), ("gy", 1)), margin)
    empty_plane = jnp.zeros_like(wide_planes[0])
    adjoint = jnp.stack(
        [wide_planes[0], empty_plane, empty_plane, wide_planes[1], empty_plane, empty_plane]
    )
    depth_now, mobility_now, inside_now = (depth_wide, mobility_wide, inside_wide)
    for _ in range(STEPS):
        adjoint = region_adjoint(adjoint, depth_now, mobility_now, inside_now)
        depth_now, mobility_now, inside_now = (
            trim_two(depth_now),
            trim_two(mobility_now),
            trim_two(inside_now),
        )
    return control + correlate(scales * adjoint, kernel, 2)


def solution(mesh):
    in_specs = (
        P(None, "gy", "gx"),
        P(),
        P("gy", "gx"),
        P("gy", "gx"),
        P(("gx", "gy"), None, None),
        P(("gx", "gy"), None, None),
        P(("gx", "gy"), None),
        P(("gx", "gy"), None, None, None),
        P(),
    )
    out_specs = P(None, "gy", "gx")
    return jax.shard_map(
        on_device, mesh=mesh, in_specs=in_specs, out_specs=out_specs, check_vma=False
    )
```

```python
import functools

import jax
import jax.numpy as jnp
from jax import lax
from jax.experimental import pallas as pl
from jax.experimental.pallas import tpu as pltpu
from jax.sharding import PartitionSpec as P

HALF = 128
BLK = 128
STEPS = 3


TIME_STEP = 0.2
GRAVITY = 1.0
FRICTION = 0.5
DIFFUSION = (0.4, 0.25)
SETTLING = (0.5, 0.2)


def band_table():
    window = jnp.arange(3 * HALF, dtype=jnp.int32)[:, None]
    column = jnp.arange(HALF, dtype=jnp.int32)[None, :]
    offsets = (window - column - HALF).astype(jnp.float32)
    corr_length = HALF / 2.0
    inside = jnp.abs(offsets) <= HALF
    kernel = jnp.where(inside, jnp.exp(-offsets * offsets / (2.0 * corr_length * corr_length)), 0.0)
    tap_offsets = jnp.arange(-HALF, HALF + 1, dtype=jnp.int32).astype(jnp.float32)
    norm_sum = jnp.sqrt(jnp.sum(jnp.exp(-tap_offsets * tap_offsets / (corr_length * corr_length))))
    return kernel / norm_sum


def split(value):
    high = value.astype(jnp.bfloat16)
    return high, (value - high.astype(jnp.float32)).astype(jnp.bfloat16)


def mul(left, right):
    return jnp.dot(left, right, preferred_element_type=jnp.float32)


def mul_pair(left, right):
    return mul(left[0], right[0]) + mul(left[0], right[1]) + mul(left[1], right[0])


def neighbours(names, counts):
    found = []
    for axis, count in zip(names, counts):
        me = lax.axis_index(axis)
        found.append((axis, me - 1, me > 0))
        found.append((axis, me + 1, me < count - 1))
    return found


def greet(around):
    barrier = pltpu.get_barrier_semaphore()
    for axis, other, there in around:

        @pl.when(there)
        def _():
            pl.semaphore_signal(
                barrier, inc=1, device_id={axis: other}, device_id_type=pl.DeviceIdType.MESH
            )

    pl.semaphore_wait(barrier, sum(there.astype(jnp.int32) for _, _, there in around))


def correlate_kernel(
    counts, x_ref, taps_ref, out_ref, low_x, high_x, low_y, high_y, wide, high_ref, low_ref, send, recv
):
    fields, rows, cols = x_ref.shape
    around = neighbours(("gx", "gy"), counts)
    greet(around)

    def taps(index):
        part = pl.ds(index * HALF, HALF)
        return high_ref[part, :], low_ref[part, :]

    def copy(field, side):
        axis, other, _ = around[side]
        if side == 0:
            source, target = x_ref.at[field], high_x.at[field]
        elif side == 1:
            source, target = x_ref.at[field], low_x.at[field]
        elif side == 2:
            source, target = wide.at[field, pl.ds(0, HALF)], high_y.at[field]
        else:
            source, target = wide.at[field, pl.ds(rows - HALF, HALF)], low_y.at[field]
        return pltpu.make_async_remote_copy(
            src_ref=source,
            dst_ref=target,
            send_sem=send.at[side, field],
            recv_sem=recv.at[side, field],
            device_id={axis: other},
            device_id_type=pl.DeviceIdType.MESH,
        )

    def start_x(field, carry):
        for side in (0, 1):

            @pl.when(around[side][2])
            def _():
                copy(field, side).start()

        return carry

    lax.fori_loop(0, fields, start_x, 0)
    for there, halo in (
        (around[0][2], low_x),
        (around[1][2], high_x),
        (around[2][2], low_y),
        (around[3][2], high_y),
    ):

        @pl.when(jnp.logical_not(there))
        def _():
            halo[...] = jnp.zeros_like(halo)

    high_ref[...], low_ref[...] = split(taps_ref[...])

    def own(field, carry):
        wide[field] = mul_pair(split(x_ref[field]), taps(1))
        return carry

    lax.fori_loop(0, fields, own, 0)

    def columns(field, carry):
        @pl.when(around[0][2])
        def _():
            copy(field, 1).wait_recv()

        @pl.when(around[1][2])
        def _():
            copy(field, 0).wait_recv()

        wide[field] = (
            wide[field]
            + mul_pair(split(low_x[field]), taps(0))
            + mul_pair(split(high_x[field]), taps(2))
        )
        for side in (2, 3):

            @pl.when(around[side][2])
            def _():
                copy(field, side).start()

        pieces = [split(wide[field, pl.ds(t * HALF, HALF), :]) for t in range(rows // HALF)]
        for t, piece in enumerate(pieces):
            total = mul_pair(taps(1), piece)
            if t > 0:
                total = total + mul_pair(taps(2), pieces[t - 1])
            if t < len(pieces) - 1:
                total = total + mul_pair(taps(0), pieces[t + 1])
            out_ref[field, pl.ds(t * HALF, HALF), :] = total
        return carry

    lax.fori_loop(0, fields, columns, 0)

    def edges(field, carry):
        @pl.when(around[2][2])
        def _():
            copy(field, 3).wait_recv()

        @pl.when(around[3][2])
        def _():
            copy(field, 2).wait_recv()

        first, last = pl.ds(0, HALF), pl.ds(rows - HALF, HALF)
        out_ref[field, first, :] = out_ref[field, first, :] + mul_pair(taps(2), split(low_y[field]))
        out_ref[field, last, :] = out_ref[field, last, :] + mul_pair(taps(0), split(high_y[field]))
        for side in range(4):

            @pl.when(around[side][2])
            def _():
                copy(field, side).wait_send()

        return carry

    lax.fori_loop(0, fields, edges, 0)


def correlate(block, kernel, name):
    fields, rows, cols = block.shape
    counts = (lax.axis_size("gx"), lax.axis_size("gy"))
    full = pl.BlockSpec(memory_space=pltpu.VMEM)
    edge = pltpu.VMEM((fields, HALF, cols), jnp.float32)
    side = pltpu.VMEM((fields, rows, cols), jnp.float32)
    return pl.pallas_call(
        functools.partial(correlate_kernel, counts),
        out_shape=jax.ShapeDtypeStruct(block.shape, jnp.float32),
        in_specs=[full] * 2,
        out_specs=full,
        scratch_shapes=[
            side,
            side,
            edge,
            edge,
            side,
            pltpu.VMEM(kernel.shape, jnp.bfloat16),
            pltpu.VMEM(kernel.shape, jnp.bfloat16),
            pltpu.SemaphoreType.DMA((4, fields)),
            pltpu.SemaphoreType.DMA((4, fields)),
        ],
        compiler_params=pltpu.CompilerParams(
            collective_id=name, has_side_effects=True, vmem_limit_bytes=40 * 2**20
        ),
        cost_estimate=pl.CostEstimate(
            flops=36 * fields * rows * cols * HALF,
            bytes_accessed=256 * fields * rows * cols,
            transcendentals=0,
        ),
    )(block, kernel)


def observation_sums(rows, footprint, instrument, live_counts, observed):
    slots = footprint.shape[1]
    live = jnp.arange(slots, dtype=jnp.int32)[None, :] < live_counts[:, None]
    code = jnp.where(live, instrument + 1, 0).astype(jnp.float32)
    code = jnp.pad(code, ((0, 0), (0, BLK - slots)))[:, None, :]
    sent = jnp.concatenate([observed, code], axis=1)
    came = lax.all_to_all(sent, ("gx", "gy"), split_axis=0, concat_axis=0, tiled=True)
    values = came[:, :slots].reshape(-1, BLK)
    kinds = came[:, slots, :slots].reshape(-1)
    here = footprint.reshape(-1)[None, :] == jnp.arange(rows, dtype=jnp.int32)[:, None]
    sums = []
    for kind in (1.0, 2.0):
        picked = (here & (kinds == kind)[None, :]).astype(jnp.float32)
        sums.append(
            (
                jnp.sum(picked, axis=1, keepdims=True),
                jnp.dot(picked, values, precision=lax.Precision.HIGHEST),
            )
        )
    return sums


CHUNK = 32
REACH = 8
PLANES = (0, 3, 1, 2, 4, 5)


def flow_kernel(
    counts, x_ref, scale_ref, depth_ref, mobility_ref, seen_ref, sums_ref, precision_ref, out_ref,
    st, pack, got, landed, send, recv,
):
    _, rows, cols = x_ref.shape
    width = 2 * cols
    around = neighbours(("gx", "gy"), counts)
    greet(around)
    base = CHUNK
    row_low, col_low = lax.axis_index("gy") * rows, lax.axis_index("gx") * cols

    def start(row):
        return pl.ds(pl.multiple_of(row, 8), CHUNK)

    for there, spot in ((around[0][2], 0), (around[1][2], 1)):

        @pl.when(jnp.logical_not(there))
        def _():
            for phase in range(2):
                got[phase, spot] = jnp.zeros((rows, cols), jnp.float32)

    def copy(phase, side):
        axis, other, _ = around[side]
        planes = 8 if phase == 0 else 2
        if side == 0:
            source, target = pack.at[phase, 0], got.at[phase, 1]
        elif side == 1:
            source, target = pack.at[phase, 1], got.at[phase, 0]
        elif side == 2:
            source = st.at[pl.ds(0, planes), pl.ds(base, REACH)]
            target = landed.at[phase, 1, pl.ds(0, planes)]
        else:
            source = st.at[pl.ds(0, planes), pl.ds(base + rows - REACH, REACH)]
            target = landed.at[phase, 0, pl.ds(0, planes)]
        return pltpu.make_async_remote_copy(
            src_ref=source,
            dst_ref=target,
            send_sem=send.at[phase, side],
            recv_sem=recv.at[phase, side],
            device_id={axis: other},
            device_id_type=pl.DeviceIdType.MESH,
        )

    def each(phase, sides, act):
        for side, way in sides:

            @pl.when(around[side][2])
            def _():
                act(copy(phase, way))

    def exchange(phase):
        planes = 8 if phase == 0 else 2
        lane = lax.broadcasted_iota(jnp.int32, (CHUNK, cols), 1)

        def fill(i, carry):
            to_low = jnp.zeros((CHUNK, cols), jnp.float32)
            to_high = to_low
            for p in range(planes):
                block = st[p, start(base + i * CHUNK), 0:cols]
                here = (lane >= REACH * p) & (lane < REACH * (p + 1))
                first = block if p == 0 else pltpu.roll(block, REACH * p, 1)
                to_low = jnp.where(here, first, to_low)
                to_high = jnp.where(here, pltpu.roll(block, REACH * p + REACH, 1), to_high)
            pack[phase, 0, start(i * CHUNK), :] = to_low
            pack[phase, 1, start(i * CHUNK), :] = to_high
            return carry

        lax.fori_loop(0, rows // CHUNK, fill, 0)
        each(phase, ((0, 0), (1, 1)), lambda c: c.start())
        each(phase, ((0, 1), (1, 0)), lambda c: c.wait_recv())

        def spread(i, carry):
            from_low = got[phase, 0, start(i * CHUNK), :]
            from_high = got[phase, 1, start(i * CHUNK), :]
            for p in range(planes):
                high = from_high if p == 0 else pltpu.roll(from_high, cols - REACH * p, 1)
                low = pltpu.roll(from_low, cols - REACH - REACH * p, 1)
                st[p, start(base + i * CHUNK), cols:width] = jnp.where(
                    lane < REACH, high, jnp.where(lane >= cols - REACH, low, 0.0)
                )
            return carry

        lax.fori_loop(0, rows // CHUNK, spread, 0)
        each(phase, ((2, 2), (3, 3)), lambda c: c.start())
        each(phase, ((2, 3), (3, 2)), lambda c: c.wait_recv())

        @pl.when(around[2][2])
        def _():
            for p in range(planes):
                st[p, pl.ds(base - REACH, REACH), :] = landed[phase, 0, p]

        @pl.when(around[3][2])
        def _():
            for p in range(planes):
                st[p, pl.ds(base + rows, REACH), :] = landed[phase, 1, p]

        each(phase, ((0, 0), (1, 1), (2, 2), (3, 3)), lambda c: c.wait_send())

    def sweep(body):
        def one(i, carry):
            row = CHUNK // 2 + i * CHUNK
            row_id = lax.broadcasted_iota(jnp.int32, (CHUNK, width), 0) + (row - base + row_low)
            lane = lax.broadcasted_iota(jnp.int32, (CHUNK, width), 1)
            col_id = jnp.where(lane < cols + cols // 2, lane, lane - width) + col_low
            inside = (
                (row_id >= 0)
                & (row_id < rows * counts[1])
                & (col_id >= 0)
                & (col_id < cols * counts[0])
            )

            def mid(p):
                return st[p, start(row), :]

            def tall(p):
                return st[p, pl.ds(pl.multiple_of(row - 8, 8), CHUNK + 16), :]

            def put(p, value):
                st[p, start(row), :] = jnp.where(inside, value, 0.0)

            body(mid, tall, put)
            return carry

        lax.fori_loop(0, (rows + CHUNK) // CHUNK, one, 0)

    def dx(value):
        return 0.5 * (pltpu.roll(value, width - 1, 1) - pltpu.roll(value, 1, 1))

    def dy(window):
        return 0.5 * (window[9 : 9 + CHUNK] - window[7 : 7 + CHUNK])

    def lap(window):
        value = window[8 : 8 + CHUNK]
        return (
            window[9 : 9 + CHUNK]
            + window[7 : 7 + CHUNK]
            + pltpu.roll(value, width - 1, 1)
            + pltpu.roll(value, 1, 1)
            - 4.0 * value
        )

    def silt(now, j, tall):
        window = tall(now + j)
        value = window[8 : 8 + CHUNK]
        return value, (
            value
            + TIME_STEP * DIFFUSION[j] * lap(window)
            - TIME_STEP * SETTLING[j] * value
        )

    for p in range(10):
        st[p] = jnp.zeros(st.shape[1:], jnp.float32)
    inner = pl.ds(base, rows)
    for p, field in enumerate(PLANES):
        st[p, inner, 0:cols] = scale_ref[field] * x_ref[field]
    st[6, inner, 0:cols] = depth_ref[...]
    st[7, inner, 0:cols] = mobility_ref[...]
    exchange(0)

    keep = 1.0 - TIME_STEP * FRICTION
    where_silt = (4, 8)
    for step in range(STEPS):
        now, later = where_silt[step % 2], where_silt[(step + 1) % 2]

        def levels(mid, tall, put):
            u, v, depth, mobility = tall(2), tall(3), tall(6), tall(7)
            part = slice(8, 8 + CHUNK)
            flow = dx(depth[part] * u[part]) + dy(depth * v)
            load = dx(mobility[part] * u[part]) + dy(mobility * v)
            one, one_new = silt(now, 0, tall)
            two, two_new = silt(now, 1, tall)
            put(0, mid(0) - TIME_STEP * flow)
            put(1, mid(1) - TIME_STEP * load + TIME_STEP * (SETTLING[0] * one + SETTLING[1] * two))
            put(later, one_new)
            put(later + 1, two_new)

        def speeds(mid, tall, put):
            surface = tall(0) + tall(1)
            put(2, keep * mid(2) - TIME_STEP * GRAVITY * dx(surface[8 : 8 + CHUNK]))
            put(3, keep * mid(3) - TIME_STEP * GRAVITY * dy(surface))

        sweep(levels)
        if step < STEPS - 1:
            sweep(speeds)

    height, bed = st[0, inner, 0:cols], st[1, inner, 0:cols]
    sar = seen_ref[0] * (height + bed) - sums_ref[0]
    lidar = seen_ref[1] * bed - sums_ref[1]
    sar = mul_pair(split(sar), split(precision_ref[0]))
    lidar = mul_pair(split(lidar), split(precision_ref[1]))
    for p in range(6):
        st[p] = jnp.zeros(st.shape[1:], jnp.float32)
    st[0, inner, 0:cols] = sar
    st[1, inner, 0:cols] = sar + lidar
    exchange(1)

    for step in range(STEPS):
        now, later = where_silt[step % 2], where_silt[(step + 1) % 2]

        def adj_levels(mid, tall, put):
            surface = TIME_STEP * GRAVITY * (dx(mid(2)) + dy(tall(3)))
            put(0, mid(0) + surface)
            put(1, mid(1) + surface)

        def adj_speeds(mid, tall, put):
            height, bed, depth, mobility = tall(0), tall(1), mid(6), mid(7)
            part = slice(8, 8 + CHUNK)
            put(2, keep * mid(2) + TIME_STEP * (depth * dx(height[part]) + mobility * dx(bed[part])))
            put(3, keep * mid(3) + TIME_STEP * (depth * dy(height) + mobility * dy(bed)))
            for j in range(2):
                _, new = silt(now, j, tall)
                put(later + j, new + TIME_STEP * SETTLING[j] * bed[part])

        if step > 0:
            sweep(adj_levels)
        sweep(adj_speeds)

    last = where_silt[STEPS % 2]
    for p, field in enumerate(PLANES):
        q = p if p < 4 else last + p - 4
        out_ref[field] = scale_ref[field] * st[q, inner, 0:cols]


def flow(block, field_scale, depth, mobility, seen, sums, obs_precision):
    _, rows, cols = block.shape
    counts = (lax.axis_size("gx"), lax.axis_size("gy"))
    full = pl.BlockSpec(memory_space=pltpu.VMEM)
    return pl.pallas_call(
        functools.partial(flow_kernel, counts),
        out_shape=jax.ShapeDtypeStruct(block.shape, jnp.float32),
        in_specs=[full, pl.BlockSpec(memory_space=pltpu.SMEM)] + [full] * 5,
        out_specs=full,
        scratch_shapes=[
            pltpu.VMEM((10, rows + 2 * CHUNK, 2 * cols), jnp.float32),
            pltpu.VMEM((2, 2, rows, cols), jnp.float32),
            pltpu.VMEM((2, 2, rows, cols), jnp.float32),
            pltpu.VMEM((2, 2, 8, REACH, 2 * cols), jnp.float32),
            pltpu.SemaphoreType.DMA((2, 4)),
            pltpu.SemaphoreType.DMA((2, 4)),
        ],
        compiler_params=pltpu.CompilerParams(
            collective_id=3, has_side_effects=True, vmem_limit_bytes=40 * 2**20
        ),
    )(block, field_scale, depth, mobility, seen, sums, obs_precision)


def on_device(
    control,
    field_scale,
    water_depth,
    bed_mobility,
    footprint,
    instrument,
    live_counts,
    observed,
    obs_precision,
):
    kernel = band_table()
    rows = water_depth.shape[0]
    (count_sar, sum_sar), (count_lidar, sum_lidar) = observation_sums(
        rows, footprint[0], instrument[0], live_counts[0], observed[0]
    )
    seen = jnp.broadcast_to(jnp.stack([count_sar, count_lidar]), (2,) + water_depth.shape)
    sums = jnp.stack([sum_sar, sum_lidar])
    smooth = correlate(control, kernel, 1)
    adjoint = flow(
        smooth, field_scale, water_depth, bed_mobility, seen, sums, obs_precision
    )
    return control + correlate(adjoint, kernel, 2)


def solution(mesh):
    in_specs = (
        P(None, "gy", "gx"),
        P(),
        P("gy", "gx"),
        P("gy", "gx"),
        P(("gx", "gy"), None, None),
        P(("gx", "gy"), None, None),
        P(("gx", "gy"), None),
        P(("gx", "gy"), None, None, None),
        P(),
    )
    out_specs = P(None, "gy", "gx")
    return jax.shard_map(
        on_device, mesh=mesh, in_specs=in_specs, out_specs=out_specs, check_vma=False
    )
```

```python
import functools

import jax
import jax.numpy as jnp
from jax import lax
from jax.experimental import pallas as pl
from jax.experimental.pallas import tpu as pltpu
from jax.sharding import PartitionSpec as P

HALF = 128
BLK = 128
STEPS = 3


TIME_STEP = 0.2
GRAVITY = 1.0
FRICTION = 0.5
DIFFUSION = (0.4, 0.25)
SETTLING = (0.5, 0.2)


def band_table():
    window = jnp.arange(3 * HALF, dtype=jnp.int32)[:, None]
    column = jnp.arange(HALF, dtype=jnp.int32)[None, :]
    offsets = (window - column - HALF).astype(jnp.float32)
    corr_length = HALF / 2.0
    inside = jnp.abs(offsets) <= HALF
    kernel = jnp.where(inside, jnp.exp(-offsets * offsets / (2.0 * corr_length * corr_length)), 0.0)
    tap_offsets = jnp.arange(-HALF, HALF + 1, dtype=jnp.int32).astype(jnp.float32)
    norm_sum = jnp.sqrt(jnp.sum(jnp.exp(-tap_offsets * tap_offsets / (corr_length * corr_length))))
    return kernel / norm_sum


def split(value):
    high = value.astype(jnp.bfloat16)
    return high, (value - high.astype(jnp.float32)).astype(jnp.bfloat16)


def mul(left, right):
    return jnp.dot(left, right, preferred_element_type=jnp.float32)


def mul_pair(left, right):
    return mul(left[0], right[0]) + mul(left[0], right[1]) + mul(left[1], right[0])


def neighbours(names, counts):
    found = []
    for axis, count in zip(names, counts):
        me = lax.axis_index(axis)
        found.append((axis, me - 1, me > 0))
        found.append((axis, me + 1, me < count - 1))
    return found


def greet(around):
    barrier = pltpu.get_barrier_semaphore()
    for axis, other, there in around:

        @pl.when(there)
        def _():
            pl.semaphore_signal(
                barrier, inc=1, device_id={axis: other}, device_id_type=pl.DeviceIdType.MESH
            )

    pl.semaphore_wait(barrier, sum(there.astype(jnp.int32) for _, _, there in around))


def correlate_kernel(
    counts, x_ref, taps_ref, out_ref, low_x, high_x, low_y, high_y, wide, high_ref, low_ref, send, recv
):
    fields, rows, cols = x_ref.shape
    around = neighbours(("gx", "gy"), counts)
    greet(around)

    def taps(index):
        part = pl.ds(index * HALF, HALF)
        return high_ref[part, :], low_ref[part, :]

    def copy(field, side):
        axis, other, _ = around[side]
        if side == 0:
            source, target = x_ref.at[field], high_x.at[field]
        elif side == 1:
            source, target = x_ref.at[field], low_x.at[field]
        elif side == 2:
            source, target = wide.at[field, pl.ds(0, HALF)], high_y.at[field]
        else:
            source, target = wide.at[field, pl.ds(rows - HALF, HALF)], low_y.at[field]
        return pltpu.make_async_remote_copy(
            src_ref=source,
            dst_ref=target,
            send_sem=send.at[side, field],
            recv_sem=recv.at[side, field],
            device_id={axis: other},
            device_id_type=pl.DeviceIdType.MESH,
        )

    def start_x(field, carry):
        for side in (0, 1):

            @pl.when(around[side][2])
            def _():
                copy(field, side).start()

        return carry

    lax.fori_loop(0, fields, start_x, 0)
    for there, halo in (
        (around[0][2], low_x),
        (around[1][2], high_x),
        (around[2][2], low_y),
        (around[3][2], high_y),
    ):

        @pl.when(jnp.logical_not(there))
        def _():
            halo[...] = jnp.zeros_like(halo)

    high_ref[...], low_ref[...] = split(taps_ref[...])

    def own(field, carry):
        wide[field] = mul_pair(split(x_ref[field]), taps(1))
        return carry

    lax.fori_loop(0, fields, own, 0)

    def columns(field, carry):
        @pl.when(around[0][2])
        def _():
            copy(field, 1).wait_recv()

        @pl.when(around[1][2])
        def _():
            copy(field, 0).wait_recv()

        wide[field] = (
            wide[field]
            + mul_pair(split(low_x[field]), taps(0))
            + mul_pair(split(high_x[field]), taps(2))
        )
        for side in (2, 3):

            @pl.when(around[side][2])
            def _():
                copy(field, side).start()

        pieces = [split(wide[field, pl.ds(t * HALF, HALF), :]) for t in range(rows // HALF)]
        for t, piece in enumerate(pieces):
            total = mul_pair(taps(1), piece)
            if t > 0:
                total = total + mul_pair(taps(2), pieces[t - 1])
            if t < len(pieces) - 1:
                total = total + mul_pair(taps(0), pieces[t + 1])
            out_ref[field, pl.ds(t * HALF, HALF), :] = total
        return carry

    lax.fori_loop(0, fields, columns, 0)

    def edges(field, carry):
        @pl.when(around[2][2])
        def _():
            copy(field, 3).wait_recv()

        @pl.when(around[3][2])
        def _():
            copy(field, 2).wait_recv()

        first, last = pl.ds(0, HALF), pl.ds(rows - HALF, HALF)
        out_ref[field, first, :] = out_ref[field, first, :] + mul_pair(taps(2), split(low_y[field]))
        out_ref[field, last, :] = out_ref[field, last, :] + mul_pair(taps(0), split(high_y[field]))
        for side in range(4):

            @pl.when(around[side][2])
            def _():
                copy(field, side).wait_send()

        return carry

    lax.fori_loop(0, fields, edges, 0)


def correlate(block, kernel, name):
    fields, rows, cols = block.shape
    counts = (lax.axis_size("gx"), lax.axis_size("gy"))
    full = pl.BlockSpec(memory_space=pltpu.VMEM)
    edge = pltpu.VMEM((fields, HALF, cols), jnp.float32)
    side = pltpu.VMEM((fields, rows, cols), jnp.float32)
    return pl.pallas_call(
        functools.partial(correlate_kernel, counts),
        out_shape=jax.ShapeDtypeStruct(block.shape, jnp.float32),
        in_specs=[full] * 2,
        out_specs=full,
        scratch_shapes=[
            side,
            side,
            edge,
            edge,
            side,
            pltpu.VMEM(kernel.shape, jnp.bfloat16),
            pltpu.VMEM(kernel.shape, jnp.bfloat16),
            pltpu.SemaphoreType.DMA((4, fields)),
            pltpu.SemaphoreType.DMA((4, fields)),
        ],
        compiler_params=pltpu.CompilerParams(
            collective_id=name, has_side_effects=True, vmem_limit_bytes=40 * 2**20
        ),
        cost_estimate=pl.CostEstimate(
            flops=36 * fields * rows * cols * HALF,
            bytes_accessed=256 * fields * rows * cols,
            transcendentals=0,
        ),
    )(block, kernel)


def observation_sums(rows, footprint, instrument, live_counts, observed):
    slots = footprint.shape[1]
    live = jnp.arange(slots, dtype=jnp.int32)[None, :] < live_counts[:, None]
    code = jnp.where(live, instrument + 1, 0).astype(jnp.float32)
    code = jnp.pad(code, ((0, 0), (0, BLK - slots)))[:, None, :]
    sent = jnp.concatenate([observed, code], axis=1)
    came = lax.all_to_all(sent, ("gx", "gy"), split_axis=0, concat_axis=0, tiled=True)
    values = came[:, :slots].reshape(-1, BLK)
    kinds = came[:, slots, :slots].reshape(-1)
    here = footprint.reshape(-1)[None, :] == jnp.arange(rows, dtype=jnp.int32)[:, None]
    sums = []
    for kind in (1.0, 2.0):
        picked = (here & (kinds == kind)[None, :]).astype(jnp.float32)
        sums.append(
            (
                jnp.sum(picked, axis=1, keepdims=True),
                jnp.dot(picked, values, precision=lax.Precision.HIGHEST),
            )
        )
    return sums


CHUNK = 32
REACH = 8
PLANES = (0, 3, 1, 2, 4, 5)


def flow_kernel(
    counts, x_ref, scale_ref, depth_ref, mobility_ref, seen_ref, sums_ref, precision_ref, out_ref,
    st, pack, got, landed, send, recv,
):
    _, rows, cols = x_ref.shape
    width = 2 * cols
    around = neighbours(("gx", "gy"), counts)
    greet(around)
    base = CHUNK
    part_rows = (rows + CHUNK) // 2
    row_low, col_low = lax.axis_index("gy") * rows, lax.axis_index("gx") * cols

    def start(row):
        return pl.ds(pl.multiple_of(row, 8), CHUNK)

    for there, spot in ((around[0][2], 0), (around[1][2], 1)):

        @pl.when(jnp.logical_not(there))
        def _():
            for phase in range(2):
                got[phase, spot] = jnp.zeros((rows, cols), jnp.float32)

    def copy(phase, side):
        axis, other, _ = around[side]
        planes = 8 if phase == 0 else 2
        if side == 0:
            source, target = pack.at[phase, 0], got.at[phase, 1]
        elif side == 1:
            source, target = pack.at[phase, 1], got.at[phase, 0]
        elif side == 2:
            source = st.at[pl.ds(0, planes), pl.ds(base, REACH)]
            target = landed.at[phase, 1, pl.ds(0, planes)]
        else:
            source = st.at[pl.ds(0, planes), pl.ds(base + rows - REACH, REACH)]
            target = landed.at[phase, 0, pl.ds(0, planes)]
        return pltpu.make_async_remote_copy(
            src_ref=source,
            dst_ref=target,
            send_sem=send.at[phase, side],
            recv_sem=recv.at[phase, side],
            device_id={axis: other},
            device_id_type=pl.DeviceIdType.MESH,
        )

    def each(phase, sides, act):
        for side, way in sides:

            @pl.when(around[side][2])
            def _():
                act(copy(phase, way))

    def exchange(phase):
        planes = 8 if phase == 0 else 2
        lane = lax.broadcasted_iota(jnp.int32, (CHUNK, cols), 1)

        def fill(i, carry):
            to_low = jnp.zeros((CHUNK, cols), jnp.float32)
            to_high = to_low
            for p in range(planes):
                block = st[p, start(base + i * CHUNK), 0:cols]
                here = (lane >= REACH * p) & (lane < REACH * (p + 1))
                first = block if p == 0 else pltpu.roll(block, REACH * p, 1)
                to_low = jnp.where(here, first, to_low)
                to_high = jnp.where(here, pltpu.roll(block, REACH * p + REACH, 1), to_high)
            pack[phase, 0, start(i * CHUNK), :] = to_low
            pack[phase, 1, start(i * CHUNK), :] = to_high
            return carry

        lax.fori_loop(0, rows // CHUNK, fill, 0)
        each(phase, ((0, 0), (1, 1)), lambda c: c.start())
        each(phase, ((0, 1), (1, 0)), lambda c: c.wait_recv())

        def spread(i, carry):
            from_low = got[phase, 0, start(i * CHUNK), :]
            from_high = got[phase, 1, start(i * CHUNK), :]
            for p in range(planes):
                high = from_high if p == 0 else pltpu.roll(from_high, cols - REACH * p, 1)
                low = pltpu.roll(from_low, cols - REACH - REACH * p, 1)
                st[p, start(base + i * CHUNK), cols:width] = jnp.where(
                    lane < REACH, high, jnp.where(lane >= cols - REACH, low, 0.0)
                )
            return carry

        lax.fori_loop(0, rows // CHUNK, spread, 0)
        each(phase, ((2, 2), (3, 3)), lambda c: c.start())
        each(phase, ((2, 3), (3, 2)), lambda c: c.wait_recv())

        @pl.when(around[2][2])
        def _():
            for p in range(planes):
                st[p, pl.ds(base - REACH, REACH), :] = landed[phase, 0, p]

        @pl.when(around[3][2])
        def _():
            for p in range(planes):
                st[p, pl.ds(base + rows, REACH), :] = landed[phase, 1, p]

        each(phase, ((0, 0), (1, 1), (2, 2), (3, 3)), lambda c: c.wait_send())

    def sweep(body):
        def one(i, carry):
            row = CHUNK // 2 + i * part_rows
            part = pl.ds(pl.multiple_of(row, 8), part_rows)
            inside = st[10, part, :]

            def mid(p):
                return st[p, part, :]

            def tall(p):
                return st[p, pl.ds(pl.multiple_of(row - 8, 8), part_rows + 16), :]

            def put(p, value):
                st[p, part, :] = value * inside

            body(mid, tall, put)
            return carry

        lax.fori_loop(0, 2, one, 0)

    def mask(i, carry):
        row = CHUNK // 2 + i * CHUNK
        row_id = lax.broadcasted_iota(jnp.int32, (CHUNK, width), 0) + (row - base + row_low)
        lane = lax.broadcasted_iota(jnp.int32, (CHUNK, width), 1)
        col_id = jnp.where(lane < cols + cols // 2, lane, lane - width) + col_low
        inside = (
            (row_id >= 0)
            & (row_id < rows * counts[1])
            & (col_id >= 0)
            & (col_id < cols * counts[0])
        )
        st[10, start(row), :] = jnp.where(inside, 1.0, 0.0)
        return carry

    def dx(value):
        return 0.5 * (pltpu.roll(value, width - 1, 1) - pltpu.roll(value, 1, 1))

    def dy(window):
        return 0.5 * (window[9 : 9 + part_rows] - window[7 : 7 + part_rows])

    def lap(window):
        value = window[8 : 8 + part_rows]
        return (
            window[9 : 9 + part_rows]
            + window[7 : 7 + part_rows]
            + pltpu.roll(value, width - 1, 1)
            + pltpu.roll(value, 1, 1)
            - 4.0 * value
        )

    def silt(now, j, tall):
        window = tall(now + j)
        value = window[8 : 8 + part_rows]
        return (
            value
            + TIME_STEP * DIFFUSION[j] * lap(window)
            - TIME_STEP * SETTLING[j] * value
        )

    for p in range(10):
        st[p] = jnp.zeros(st.shape[1:], jnp.float32)
    inner = pl.ds(base, rows)
    for p, field in enumerate(PLANES):
        st[p, inner, 0:cols] = scale_ref[field] * x_ref[field]
    st[6, inner, 0:cols] = depth_ref[...]
    st[7, inner, 0:cols] = mobility_ref[...]
    lax.fori_loop(0, (rows + CHUNK) // CHUNK, mask, 0)
    exchange(0)

    keep = 1.0 - TIME_STEP * FRICTION
    where_silt = (4, 8)
    for step in range(STEPS):
        now, later = where_silt[step % 2], where_silt[(step + 1) % 2]

        def levels(mid, tall, put):
            u, v, depth, mobility = tall(2), tall(3), tall(6), tall(7)
            part = slice(8, 8 + part_rows)
            flow = dx(depth[part] * u[part]) + dy(depth * v)
            load = dx(mobility[part] * u[part]) + dy(mobility * v)
            one, two = mid(now), mid(now + 1)
            put(0, mid(0) - TIME_STEP * flow)
            put(1, mid(1) - TIME_STEP * load + TIME_STEP * (SETTLING[0] * one + SETTLING[1] * two))
            if step < STEPS - 1:
                for j in range(2):
                    put(later + j, silt(now, j, tall))

        def speeds(mid, tall, put):
            surface = tall(0) + tall(1)
            put(2, keep * mid(2) - TIME_STEP * GRAVITY * dx(surface[8 : 8 + part_rows]))
            put(3, keep * mid(3) - TIME_STEP * GRAVITY * dy(surface))

        sweep(levels)
        if step < STEPS - 1:
            sweep(speeds)

    height, bed = st[0, inner, 0:cols], st[1, inner, 0:cols]
    sar = seen_ref[0] * (height + bed) - sums_ref[0]
    lidar = seen_ref[1] * bed - sums_ref[1]
    sar = mul_pair(split(sar), split(precision_ref[0]))
    lidar = mul_pair(split(lidar), split(precision_ref[1]))
    for p in range(6):
        st[p] = jnp.zeros(st.shape[1:], jnp.float32)
    st[0, inner, 0:cols] = sar
    st[1, inner, 0:cols] = sar + lidar
    exchange(1)

    for step in range(STEPS):
        now, later = where_silt[step % 2], where_silt[(step + 1) % 2]

        def adj_levels(mid, tall, put):
            surface = TIME_STEP * GRAVITY * (dx(mid(2)) + dy(tall(3)))
            put(0, mid(0) + surface)
            put(1, mid(1) + surface)

        def adj_speeds(mid, tall, put):
            height, bed, depth, mobility = tall(0), tall(1), mid(6), mid(7)
            part = slice(8, 8 + part_rows)
            push_x = TIME_STEP * (depth * dx(height[part]) + mobility * dx(bed[part]))
            push_y = TIME_STEP * (depth * dy(height) + mobility * dy(bed))
            put(2, push_x if step == 0 else keep * mid(2) + push_x)
            put(3, push_y if step == 0 else keep * mid(3) + push_y)
            for j in range(2):
                gain = TIME_STEP * SETTLING[j] * bed[part]
                put(later + j, gain if step == 0 else silt(now, j, tall) + gain)

        if step > 0:
            sweep(adj_levels)
        sweep(adj_speeds)

    last = where_silt[STEPS % 2]
    for p, field in enumerate(PLANES):
        q = p if p < 4 else last + p - 4
        out_ref[field] = scale_ref[field] * st[q, inner, 0:cols]


def flow(block, field_scale, depth, mobility, seen, sums, obs_precision):
    _, rows, cols = block.shape
    counts = (lax.axis_size("gx"), lax.axis_size("gy"))
    full = pl.BlockSpec(memory_space=pltpu.VMEM)
    return pl.pallas_call(
        functools.partial(flow_kernel, counts),
        out_shape=jax.ShapeDtypeStruct(block.shape, jnp.float32),
        in_specs=[full, pl.BlockSpec(memory_space=pltpu.SMEM)] + [full] * 5,
        out_specs=full,
        scratch_shapes=[
            pltpu.VMEM((11, rows + 2 * CHUNK, 2 * cols), jnp.float32),
            pltpu.VMEM((2, 2, rows, cols), jnp.float32),
            pltpu.VMEM((2, 2, rows, cols), jnp.float32),
            pltpu.VMEM((2, 2, 8, REACH, 2 * cols), jnp.float32),
            pltpu.SemaphoreType.DMA((2, 4)),
            pltpu.SemaphoreType.DMA((2, 4)),
        ],
        compiler_params=pltpu.CompilerParams(
            collective_id=3, has_side_effects=True, vmem_limit_bytes=40 * 2**20
        ),
    )(block, field_scale, depth, mobility, seen, sums, obs_precision)


def on_device(
    control,
    field_scale,
    water_depth,
    bed_mobility,
    footprint,
    instrument,
    live_counts,
    observed,
    obs_precision,
):
    kernel = band_table()
    rows = water_depth.shape[0]
    (count_sar, sum_sar), (count_lidar, sum_lidar) = observation_sums(
        rows, footprint[0], instrument[0], live_counts[0], observed[0]
    )
    seen = jnp.broadcast_to(jnp.stack([count_sar, count_lidar]), (2,) + water_depth.shape)
    sums = jnp.stack([sum_sar, sum_lidar])
    smooth = correlate(control, kernel, 1)
    adjoint = flow(
        smooth, field_scale, water_depth, bed_mobility, seen, sums, obs_precision
    )
    return control + correlate(adjoint, kernel, 2)


def solution(mesh):
    in_specs = (
        P(None, "gy", "gx"),
        P(),
        P("gy", "gx"),
        P("gy", "gx"),
        P(("gx", "gy"), None, None),
        P(("gx", "gy"), None, None),
        P(("gx", "gy"), None),
        P(("gx", "gy"), None, None, None),
        P(),
    )
    out_specs = P(None, "gy", "gx")
    return jax.shard_map(
        on_device, mesh=mesh, in_specs=in_specs, out_specs=out_specs, check_vma=False
    )
```

```python
import functools

import jax
import jax.numpy as jnp
from jax import lax
from jax.experimental import pallas as pl
from jax.experimental.pallas import tpu as pltpu
from jax.sharding import PartitionSpec as P

HALF = 128
BLK = 128
STEPS = 3


TIME_STEP = 0.2
GRAVITY = 1.0
FRICTION = 0.5
DIFFUSION = (0.4, 0.25)
SETTLING = (0.5, 0.2)


def band_table():
    window = jnp.arange(3 * HALF, dtype=jnp.int32)[:, None]
    column = jnp.arange(HALF, dtype=jnp.int32)[None, :]
    offsets = (window - column - HALF).astype(jnp.float32)
    corr_length = HALF / 2.0
    inside = jnp.abs(offsets) <= HALF
    kernel = jnp.where(inside, jnp.exp(-offsets * offsets / (2.0 * corr_length * corr_length)), 0.0)
    tap_offsets = jnp.arange(-HALF, HALF + 1, dtype=jnp.int32).astype(jnp.float32)
    norm_sum = jnp.sqrt(jnp.sum(jnp.exp(-tap_offsets * tap_offsets / (corr_length * corr_length))))
    return kernel / norm_sum


def split(value):
    high = value.astype(jnp.bfloat16)
    return high, (value - high.astype(jnp.float32)).astype(jnp.bfloat16)


def mul(left, right):
    return jnp.dot(left, right, preferred_element_type=jnp.float32)


def mul_pair(left, right):
    return mul(left[0], right[0]) + mul(left[0], right[1]) + mul(left[1], right[0])


def neighbours(names, counts):
    found = []
    for axis, count in zip(names, counts):
        me = lax.axis_index(axis)
        found.append((axis, me - 1, me > 0))
        found.append((axis, me + 1, me < count - 1))
    return found


def greet(around):
    barrier = pltpu.get_barrier_semaphore()
    for axis, other, there in around:

        @pl.when(there)
        def _():
            pl.semaphore_signal(
                barrier, inc=1, device_id={axis: other}, device_id_type=pl.DeviceIdType.MESH
            )

    pl.semaphore_wait(barrier, sum(there.astype(jnp.int32) for _, _, there in around))


def correlate_kernel(
    counts, x_ref, taps_ref, out_ref, low_x, high_x, low_y, high_y, wide, high_ref, low_ref, send, recv
):
    fields, rows, cols = x_ref.shape
    around = neighbours(("gx", "gy"), counts)
    greet(around)

    def taps(index):
        part = pl.ds(index * HALF, HALF)
        return high_ref[part, :], low_ref[part, :]

    def copy(field, side):
        axis, other, _ = around[side]
        if side == 0:
            source, target = x_ref.at[field], high_x.at[field]
        elif side == 1:
            source, target = x_ref.at[field], low_x.at[field]
        elif side == 2:
            source, target = wide.at[field, pl.ds(0, HALF)], high_y.at[field]
        else:
            source, target = wide.at[field, pl.ds(rows - HALF, HALF)], low_y.at[field]
        return pltpu.make_async_remote_copy(
            src_ref=source,
            dst_ref=target,
            send_sem=send.at[side, field],
            recv_sem=recv.at[side, field],
            device_id={axis: other},
            device_id_type=pl.DeviceIdType.MESH,
        )

    def start_x(field, carry):
        for side in (0, 1):

            @pl.when(around[side][2])
            def _():
                copy(field, side).start()

        return carry

    lax.fori_loop(0, fields, start_x, 0)
    for there, halo in (
        (around[0][2], low_x),
        (around[1][2], high_x),
        (around[2][2], low_y),
        (around[3][2], high_y),
    ):

        @pl.when(jnp.logical_not(there))
        def _():
            halo[...] = jnp.zeros_like(halo)

    high_ref[...], low_ref[...] = split(taps_ref[...])

    def own(field, carry):
        wide[field] = mul_pair(split(x_ref[field]), taps(1))
        return carry

    lax.fori_loop(0, fields, own, 0)

    def columns(field, carry):
        @pl.when(around[0][2])
        def _():
            copy(field, 1).wait_recv()

        @pl.when(around[1][2])
        def _():
            copy(field, 0).wait_recv()

        wide[field] = (
            wide[field]
            + mul_pair(split(low_x[field]), taps(0))
            + mul_pair(split(high_x[field]), taps(2))
        )
        for side in (2, 3):

            @pl.when(around[side][2])
            def _():
                copy(field, side).start()

        pieces = [split(wide[field, pl.ds(t * HALF, HALF), :]) for t in range(rows // HALF)]
        for t, piece in enumerate(pieces):
            total = mul_pair(taps(1), piece)
            if t > 0:
                total = total + mul_pair(taps(2), pieces[t - 1])
            if t < len(pieces) - 1:
                total = total + mul_pair(taps(0), pieces[t + 1])
            out_ref[field, pl.ds(t * HALF, HALF), :] = total
        return carry

    lax.fori_loop(0, fields, columns, 0)

    def edges(field, carry):
        @pl.when(around[2][2])
        def _():
            copy(field, 3).wait_recv()

        @pl.when(around[3][2])
        def _():
            copy(field, 2).wait_recv()

        first, last = pl.ds(0, HALF), pl.ds(rows - HALF, HALF)
        out_ref[field, first, :] = out_ref[field, first, :] + mul_pair(taps(2), split(low_y[field]))
        out_ref[field, last, :] = out_ref[field, last, :] + mul_pair(taps(0), split(high_y[field]))
        for side in range(4):

            @pl.when(around[side][2])
            def _():
                copy(field, side).wait_send()

        return carry

    lax.fori_loop(0, fields, edges, 0)


def correlate(block, kernel, name):
    fields, rows, cols = block.shape
    counts = (lax.axis_size("gx"), lax.axis_size("gy"))
    full = pl.BlockSpec(memory_space=pltpu.VMEM)
    edge = pltpu.VMEM((fields, HALF, cols), jnp.float32)
    side = pltpu.VMEM((fields, rows, cols), jnp.float32)
    return pl.pallas_call(
        functools.partial(correlate_kernel, counts),
        out_shape=jax.ShapeDtypeStruct(block.shape, jnp.float32),
        in_specs=[full] * 2,
        out_specs=full,
        scratch_shapes=[
            side,
            side,
            edge,
            edge,
            side,
            pltpu.VMEM(kernel.shape, jnp.bfloat16),
            pltpu.VMEM(kernel.shape, jnp.bfloat16),
            pltpu.SemaphoreType.DMA((4, fields)),
            pltpu.SemaphoreType.DMA((4, fields)),
        ],
        compiler_params=pltpu.CompilerParams(
            collective_id=name, has_side_effects=True, vmem_limit_bytes=40 * 2**20
        ),
        cost_estimate=pl.CostEstimate(
            flops=36 * fields * rows * cols * HALF,
            bytes_accessed=256 * fields * rows * cols,
            transcendentals=0,
        ),
    )(block, kernel)


def observation_sums(rows, footprint, instrument, live_counts, observed):
    slots = footprint.shape[1]
    live = jnp.arange(slots, dtype=jnp.int32)[None, :] < live_counts[:, None]
    code = jnp.where(live, instrument + 1, 0).astype(jnp.float32)
    code = jnp.pad(code, ((0, 0), (0, BLK - slots)))[:, None, :]
    sent = jnp.concatenate([observed, code], axis=1)
    came = lax.all_to_all(sent, ("gx", "gy"), split_axis=0, concat_axis=0, tiled=True)
    values = came[:, :slots].reshape(-1, BLK)
    kinds = came[:, slots, :slots].reshape(-1)
    here = footprint.reshape(-1)[None, :] == jnp.arange(rows, dtype=jnp.int32)[:, None]
    sums = []
    for kind in (1.0, 2.0):
        picked = (here & (kinds == kind)[None, :]).astype(jnp.float32)
        sums.append(
            (
                jnp.sum(picked, axis=1, keepdims=True),
                jnp.dot(picked, values, precision=lax.Precision.HIGHEST),
            )
        )
    return sums


CHUNK = 32
REACH = 8
PLANES = (0, 3, 1, 2, 4, 5)


def flow_kernel(
    counts, x_ref, scale_ref, depth_ref, mobility_ref, seen_ref, sums_ref, precision_ref, out_ref,
    st, pack, got, landed, send, recv,
):
    _, rows, cols = x_ref.shape
    width = 2 * cols
    around = neighbours(("gx", "gy"), counts)
    greet(around)
    base = CHUNK
    part_rows = (rows + CHUNK) // 2
    row_low, col_low = lax.axis_index("gy") * rows, lax.axis_index("gx") * cols

    def start(row):
        return pl.ds(pl.multiple_of(row, 8), CHUNK)

    for there, spot in ((around[0][2], 0), (around[1][2], 1)):

        @pl.when(jnp.logical_not(there))
        def _():
            for phase in range(2):
                got[phase, spot] = jnp.zeros((rows, cols), jnp.float32)

    def copy(phase, side):
        axis, other, _ = around[side]
        planes = 8 if phase == 0 else 2
        if side == 0:
            source, target = pack.at[phase, 0], got.at[phase, 1]
        elif side == 1:
            source, target = pack.at[phase, 1], got.at[phase, 0]
        elif side == 2:
            source = st.at[pl.ds(0, planes), pl.ds(base, REACH)]
            target = landed.at[phase, 1, pl.ds(0, planes)]
        else:
            source = st.at[pl.ds(0, planes), pl.ds(base + rows - REACH, REACH)]
            target = landed.at[phase, 0, pl.ds(0, planes)]
        return pltpu.make_async_remote_copy(
            src_ref=source,
            dst_ref=target,
            send_sem=send.at[phase, side],
            recv_sem=recv.at[phase, side],
            device_id={axis: other},
            device_id_type=pl.DeviceIdType.MESH,
        )

    def each(phase, sides, act):
        for side, way in sides:

            @pl.when(around[side][2])
            def _():
                act(copy(phase, way))

    band = rows // 4

    def piece(row):
        return pl.ds(pl.multiple_of(row, 8), band)

    def exchange(phase):
        planes = 8 if phase == 0 else 2
        lane = lax.broadcasted_iota(jnp.int32, (band, cols), 1)

        def fill(i, carry):
            to_low = jnp.zeros((band, cols), jnp.float32)
            to_high = to_low
            for p in range(planes):
                block = st[p, piece(base + i * band), 0:cols]
                here = (lane >= REACH * p) & (lane < REACH * (p + 1))
                first = block if p == 0 else pltpu.roll(block, REACH * p, 1)
                to_low = jnp.where(here, first, to_low)
                to_high = jnp.where(here, pltpu.roll(block, REACH * p + REACH, 1), to_high)
            pack[phase, 0, piece(i * band), :] = to_low
            pack[phase, 1, piece(i * band), :] = to_high
            return carry

        lax.fori_loop(0, 4, fill, 0)
        each(phase, ((0, 0), (1, 1)), lambda c: c.start())
        each(phase, ((0, 1), (1, 0)), lambda c: c.wait_recv())

        def spread(i, carry):
            from_low = got[phase, 0, piece(i * band), :]
            from_high = got[phase, 1, piece(i * band), :]
            for p in range(planes):
                high = from_high if p == 0 else pltpu.roll(from_high, cols - REACH * p, 1)
                low = pltpu.roll(from_low, cols - REACH - REACH * p, 1)
                st[p, piece(base + i * band), cols:width] = jnp.where(
                    lane < REACH, high, jnp.where(lane >= cols - REACH, low, 0.0)
                )
            return carry

        lax.fori_loop(0, 4, spread, 0)
        each(phase, ((2, 2), (3, 3)), lambda c: c.start())
        each(phase, ((2, 3), (3, 2)), lambda c: c.wait_recv())

        @pl.when(around[2][2])
        def _():
            for p in range(planes):
                st[p, pl.ds(base - REACH, REACH), :] = landed[phase, 0, p]

        @pl.when(around[3][2])
        def _():
            for p in range(planes):
                st[p, pl.ds(base + rows, REACH), :] = landed[phase, 1, p]

        each(phase, ((0, 0), (1, 1), (2, 2), (3, 3)), lambda c: c.wait_send())

    def sweep(body):
        def one(i, carry):
            row = CHUNK // 2 + i * part_rows
            part = pl.ds(pl.multiple_of(row, 8), part_rows)
            inside = st[10, part, :]

            def mid(p):
                return st[p, part, :]

            def tall(p):
                return st[p, pl.ds(pl.multiple_of(row - 8, 8), part_rows + 16), :]

            def put(p, value):
                st[p, part, :] = value * inside

            body(mid, tall, put)
            return carry

        lax.fori_loop(0, 2, one, 0)

    def mask(i, carry):
        row = CHUNK // 2 + i * CHUNK
        row_id = lax.broadcasted_iota(jnp.int32, (CHUNK, width), 0) + (row - base + row_low)
        lane = lax.broadcasted_iota(jnp.int32, (CHUNK, width), 1)
        col_id = jnp.where(lane < cols + cols // 2, lane, lane - width) + col_low
        inside = (
            (row_id >= 0)
            & (row_id < rows * counts[1])
            & (col_id >= 0)
            & (col_id < cols * counts[0])
        )
        st[10, start(row), :] = jnp.where(inside, 1.0, 0.0)
        return carry

    def dx(value):
        return 0.5 * (pltpu.roll(value, width - 1, 1) - pltpu.roll(value, 1, 1))

    def dy(window):
        return 0.5 * (window[9 : 9 + part_rows] - window[7 : 7 + part_rows])

    def lap(window):
        value = window[8 : 8 + part_rows]
        return (
            window[9 : 9 + part_rows]
            + window[7 : 7 + part_rows]
            + pltpu.roll(value, width - 1, 1)
            + pltpu.roll(value, 1, 1)
            - 4.0 * value
        )

    def silt(now, j, tall):
        window = tall(now + j)
        value = window[8 : 8 + part_rows]
        return (
            value
            + TIME_STEP * DIFFUSION[j] * lap(window)
            - TIME_STEP * SETTLING[j] * value
        )

    for p in range(10):
        st[p] = jnp.zeros(st.shape[1:], jnp.float32)
    inner = pl.ds(base, rows)
    for p, field in enumerate(PLANES):
        st[p, inner, 0:cols] = scale_ref[field] * x_ref[field]
    st[6, inner, 0:cols] = depth_ref[...]
    st[7, inner, 0:cols] = mobility_ref[...]
    lax.fori_loop(0, (rows + CHUNK) // CHUNK, mask, 0)
    exchange(0)

    keep = 1.0 - TIME_STEP * FRICTION
    where_silt = (4, 8)
    for step in range(STEPS):
        now, later = where_silt[step % 2], where_silt[(step + 1) % 2]

        def levels(mid, tall, put):
            u, v, depth, mobility = tall(2), tall(3), tall(6), tall(7)
            part = slice(8, 8 + part_rows)
            flow = dx(depth[part] * u[part]) + dy(depth * v)
            load = dx(mobility[part] * u[part]) + dy(mobility * v)
            one, two = mid(now), mid(now + 1)
            put(0, mid(0) - TIME_STEP * flow)
            put(1, mid(1) - TIME_STEP * load + TIME_STEP * (SETTLING[0] * one + SETTLING[1] * two))
            if step < STEPS - 1:
                for j in range(2):
                    put(later + j, silt(now, j, tall))

        def speeds(mid, tall, put):
            surface = tall(0) + tall(1)
            put(2, keep * mid(2) - TIME_STEP * GRAVITY * dx(surface[8 : 8 + part_rows]))
            put(3, keep * mid(3) - TIME_STEP * GRAVITY * dy(surface))

        sweep(levels)
        if step < STEPS - 1:
            sweep(speeds)

    height, bed = st[0, inner, 0:cols], st[1, inner, 0:cols]
    sar = seen_ref[0] * (height + bed) - sums_ref[0]
    lidar = seen_ref[1] * bed - sums_ref[1]
    sar = mul_pair(split(sar), split(precision_ref[0]))
    lidar = mul_pair(split(lidar), split(precision_ref[1]))
    for p in range(6):
        st[p] = jnp.zeros(st.shape[1:], jnp.float32)
    st[0, inner, 0:cols] = sar
    st[1, inner, 0:cols] = sar + lidar
    exchange(1)

    for step in range(STEPS):
        now, later = where_silt[step % 2], where_silt[(step + 1) % 2]

        def adj_levels(mid, tall, put):
            surface = TIME_STEP * GRAVITY * (dx(mid(2)) + dy(tall(3)))
            put(0, mid(0) + surface)
            put(1, mid(1) + surface)

        def adj_speeds(mid, tall, put):
            height, bed, depth, mobility = tall(0), tall(1), mid(6), mid(7)
            part = slice(8, 8 + part_rows)
            push_x = TIME_STEP * (depth * dx(height[part]) + mobility * dx(bed[part]))
            push_y = TIME_STEP * (depth * dy(height) + mobility * dy(bed))
            put(2, push_x if step == 0 else keep * mid(2) + push_x)
            put(3, push_y if step == 0 else keep * mid(3) + push_y)
            for j in range(2):
                gain = TIME_STEP * SETTLING[j] * bed[part]
                put(later + j, gain if step == 0 else silt(now, j, tall) + gain)

        if step > 0:
            sweep(adj_levels)
        sweep(adj_speeds)

    last = where_silt[STEPS % 2]
    for p, field in enumerate(PLANES):
        q = p if p < 4 else last + p - 4
        out_ref[field] = scale_ref[field] * st[q, inner, 0:cols]


def flow(block, field_scale, depth, mobility, seen, sums, obs_precision):
    _, rows, cols = block.shape
    counts = (lax.axis_size("gx"), lax.axis_size("gy"))
    full = pl.BlockSpec(memory_space=pltpu.VMEM)
    return pl.pallas_call(
        functools.partial(flow_kernel, counts),
        out_shape=jax.ShapeDtypeStruct(block.shape, jnp.float32),
        in_specs=[full, pl.BlockSpec(memory_space=pltpu.SMEM)] + [full] * 5,
        out_specs=full,
        scratch_shapes=[
            pltpu.VMEM((11, rows + 2 * CHUNK, 2 * cols), jnp.float32),
            pltpu.VMEM((2, 2, rows, cols), jnp.float32),
            pltpu.VMEM((2, 2, rows, cols), jnp.float32),
            pltpu.VMEM((2, 2, 8, REACH, 2 * cols), jnp.float32),
            pltpu.SemaphoreType.DMA((2, 4)),
            pltpu.SemaphoreType.DMA((2, 4)),
        ],
        compiler_params=pltpu.CompilerParams(
            collective_id=3, has_side_effects=True, vmem_limit_bytes=40 * 2**20
        ),
    )(block, field_scale, depth, mobility, seen, sums, obs_precision)


def on_device(
    control,
    field_scale,
    water_depth,
    bed_mobility,
    footprint,
    instrument,
    live_counts,
    observed,
    obs_precision,
):
    kernel = band_table()
    rows = water_depth.shape[0]
    (count_sar, sum_sar), (count_lidar, sum_lidar) = observation_sums(
        rows, footprint[0], instrument[0], live_counts[0], observed[0]
    )
    seen = jnp.broadcast_to(jnp.stack([count_sar, count_lidar]), (2,) + water_depth.shape)
    sums = jnp.stack([sum_sar, sum_lidar])
    smooth = correlate(control, kernel, 1)
    adjoint = flow(
        smooth, field_scale, water_depth, bed_mobility, seen, sums, obs_precision
    )
    return control + correlate(adjoint, kernel, 2)


def solution(mesh):
    in_specs = (
        P(None, "gy", "gx"),
        P(),
        P("gy", "gx"),
        P("gy", "gx"),
        P(("gx", "gy"), None, None),
        P(("gx", "gy"), None, None),
        P(("gx", "gy"), None),
        P(("gx", "gy"), None, None, None),
        P(),
    )
    out_specs = P(None, "gy", "gx")
    return jax.shard_map(
        on_device, mesh=mesh, in_specs=in_specs, out_specs=out_specs, check_vma=False
    )
```
